32 devices in a mesh: grp: 2 (over y), ex: 4 (over z), lyr: 4 (over x, core).
Axes of the slice: x: 2, y: 2, z: 4, core: 2. Of those that a mesh axis runs over, the one named last changes fastest.
Arguments:
- train_grads: bfloat16 [4, 4096, 4096], P('lyr', ('grp', 'ex')), parts along dimension 1, may hold values from -6 to 6
- query_grads: bfloat16 [4, 128, 4096], P('lyr', 'ex'), may hold values from -6 to 6
- basis_out: float32 [4, 64, 64], P('lyr'), may hold values from -0.75 to 0.75
- basis_in: float32 [4, 64, 64], P('lyr'), may hold values from -0.75 to 0.75
- eigenvalues: float32 [4, 4096], P('lyr'), may hold values from 0.05 to 5
Outputs:
- scores: float32 [4096, 128], P(('grp', 'ex'), 'lyr'), parts along dimension 0
The draws below stay inside these ranges and needn't reach their ends.
There are 2 independent parts, one for each index of `grp`. The reference program is written for one: setup_inputs(seed, part) draws one part's arguments, and reference() takes and returns one part's arrays. A program takes and returns all parts, laid end to end along the dimension named above; an argument that names none is the same for every part. Nothing has to cross between parts.
All inputs are finite; a program needn't handle non-finite values.
Results may differ from the reference program's by a relative error of at most 0.0029.
Values may be sent and summed in bfloat16 or wider, within the bound.
No kernel may reach another device: no remote copies, remote signals or barrier semaphores. Data moves between devices by JAX's collectives and lax.ppermute only.
A program may use at most 64 MiB of HBM per device.

```python
import math
import jax
import jax.numpy as jnp
from jax import lax

GR = 64
GC = 64
LAYERS = 4
NTRAIN = 2048
NQ = 128


def block_levels(key, extent, pieces, smallest, largest):
    factor_of = 1.0
    for position, blocks in pieces:
        heights = jax.random.uniform(jax.random.fold_in(jax.random.fold_in(key, 6), position), (blocks,), jnp.float32, smallest / len(pieces), largest / len(pieces))
        factor_of = factor_of * jnp.repeat(jnp.exp(heights), extent[position] // blocks).reshape((-1,) + (1,) * (len(extent) - 1 - position))
    return factor_of


def scatter_about(rng, shape, spread, bound, shards=(), held_as=jnp.bfloat16):
    array = jax.random.normal(rng, shape, jnp.float32) * spread
    if len(shards) > 0:
        array = block_levels(rng, shape, shards, -0.22, 0.18) * array
    return jnp.clip(array, min=-bound, max=bound).astype(held_as)


def setup_inputs(seed: int = 0, part: int = 0) -> dict:
    key_list = jax.random.split(jax.random.key(seed), 6)
    part_splits = jax.random.split(jax.random.fold_in(key_list[5], part), 6)
    return {
        "train_grads": scatter_about(part_splits[0], (LAYERS, NTRAIN, GR * GC), 1.0, 6.0, ((0, 4), (1, 4))),
        "query_grads": scatter_about(key_list[1], (LAYERS, NQ, GR * GC), 1.0, 6.0, ((0, 4), (1, 4))),
        "basis_out": scatter_about(key_list[2], (LAYERS, GR, GR), GR ** -0.5, 0.75, ((0, 4),), jnp.float32),
        "basis_in": scatter_about(key_list[3], (LAYERS, GC, GC), GC ** -0.5, 0.75, ((0, 4),), jnp.float32),
        "eigenvalues": jnp.clip(jnp.exp(math.log(5.0) - 4.6051702 * jax.random.uniform(key_list[4], (LAYERS, GR * GC), jnp.float32) ** block_levels(key_list[4], (LAYERS, GR * GC), ((0, 4),), -0.2, 0.2)), 0.05, 5.0),
    }


damping = 0.1

def prepare(grads, basis_out, basis_in, eigenvalues):
    layers, count, width = grads.shape
    rows_out = basis_out.shape[1]
    cols_in = basis_in.shape[1]
    matrix = grads.astype(jnp.float32).reshape(layers, count, rows_out, cols_in)
    rotated = jnp.einsum('lba,lqbc->lqac', basis_out, matrix, precision=lax.Precision.HIGHEST)
    rotated = jnp.einsum('lqac,lcd->lqad', rotated, basis_in, precision=lax.Precision.HIGHEST)
    scaled = rotated / (eigenvalues.reshape(layers, 1, rows_out, cols_in) + damping)
    back = jnp.einsum('lab,lqbc->lqac', basis_out, scaled, precision=lax.Precision.HIGHEST)
    back = jnp.einsum('lqac,ldc->lqad', back, basis_in, precision=lax.Precision.HIGHEST)
    return back.reshape(layers, count, width).astype(jnp.bfloat16)

def reference(train_grads, query_grads, basis_out, basis_in, eigenvalues):
    ready = prepare(query_grads, basis_out, basis_in, eigenvalues)
    total = jnp.zeros((NTRAIN, NQ), jnp.float32)
    for layer in range(LAYERS):
        total = total + jnp.dot(train_grads[layer], ready[layer].T, preferred_element_type=jnp.float32)
    return total / math.sqrt(GR * GC)
```

```python
import functools
import math

import jax, jax.numpy as jnp
from jax import lax
from jax.experimental import pallas as pl
from jax.experimental.pallas import tpu as pltpu
from jax.sharding import PartitionSpec as P

GR = 64
GC = 64
damping = 0.1
F32, BF16 = jnp.float32, jnp.bfloat16


def dot(a, b, ca=1, cb=0):
    return lax.dot_general(a, b, (((ca,), (cb,)), ((), ())), preferred_element_type=F32)
def split(x):
    h = x.astype(BF16)
    return h, (x - h.astype(F32)).astype(BF16)
def selector(rows, which, swap):
    k = lax.broadcasted_iota(jnp.int32, (rows, 64), 0)
    b = lax.broadcasted_iota(jnp.int32, (rows, 64), 1)
    kk = k % 64
    par = kk // 32
    if swap: par = 1 - par
    hit = b == 2 * (kk % 32) + par
    if which == 1: hit = hit & (k < 128)
    if which == 2: hit = hit & (k >= 128)
    return jnp.where(hit, 1.0, 0.0).astype(BF16)
def row_maps(bo):
    h, l = split(bo)
    sel = selector(64, 0, False)
    outs = []
    for cb in (1, 0):
        th, tl = dot(sel, h, 1, cb).astype(BF16), dot(sel, l, 1, cb).astype(BF16)
        parts = []
        for swap in (False, True):
            full = dot(th, selector(192, 1, swap), 1, 1) + dot(tl, selector(192, 2, swap), 1, 1)
            parts.append(full[32 * swap:32 * swap + 32])
        outs.append(jnp.concatenate(parts, 0).astype(BF16))
    return outs
def col_maps(bi):
    h, l = split(bi)
    r = lax.broadcasted_iota(jnp.int32, (128, 64), 0) % 64
    c = lax.broadcasted_iota(jnp.int32, (128, 64), 1)
    e = jnp.where(r == c, 1.0, 0.0).astype(BF16)
    i = lax.broadcasted_iota(jnp.int32, (128, 128), 0) // 64
    j = lax.broadcasted_iota(jnp.int32, (128, 128), 1) // 64
    same = i == j
    def tile(x, cb):
        t = dot(e, x, 1, cb).astype(BF16)
        return dot(t, e, 1, 1)
    def pick(t, m): return jnp.where(m, t, 0.0).astype(BF16)
    th, tl = tile(h, 0), tile(l, 0)
    diff = jnp.logical_not(same)
    first = jnp.concatenate([jnp.concatenate([pick(th, same), pick(th, diff)], 1), jnp.concatenate([pick(tl, same), pick(tl, diff)], 1)], 0)
    uh, ul = tile(h, 1), tile(l, 1)
    last = jnp.concatenate([pick(uh, same), pick(uh, same), pick(ul, same)], 0)
    return first, last
def prep_body(nq, get, put, left_in, left_out, first, last, rec, xa, xb, os, group=8):
    g = jnp.concatenate([get(t) for t in range(32)], 0)
    x = dot(jnp.concatenate([g, g], 1), first)
    xa[...] = x[:, :128]
    xb[...] = x[:, 128:]
    lane = lax.broadcasted_iota(jnp.int32, (32, 128), 1) < 64
    for q0 in range(0, nq, group):
        qs = range(q0, q0 + group)
        ww = jnp.concatenate([jnp.concatenate([r[pl.ds(q, 32, stride=nq), :] for q in qs], 1) for r in (xa, xb)], 0)
        h, l = split(ww)
        r = dot(left_in, jnp.concatenate([h, l, h], 0))
        ys, yr = [], []
        for i in range(group):
            s = slice(i * 128, i * 128 + 128)
            y = jnp.where(lane, r[:32, s], r[32:, s]) * rec
            ys.append(y); yr.append(pltpu.roll(y, 64, 1))
        yy = jnp.concatenate([jnp.concatenate(ys, 1), jnp.concatenate(yr, 1)], 0)
        h, l = split(yy)
        r = dot(left_out, jnp.concatenate([h, l, h], 0))
        z = jnp.concatenate([jnp.where(lane, r[:32, i * 128:i * 128 + 128], r[32:, i * 128:i * 128 + 128]) for i in range(group)], 0)
        h, l = split(z)
        os[pl.ds(q0 * 32, group * 32), :] = dot(jnp.concatenate([h, l, h], 1), last)
    for t in range(32):
        put(t, os[pl.ds(t, nq, stride=32), :])

def prep_kernel(nq, group, q_hbm, bo_hbm, bi_hbm, ev_hbm, o_ref, qv, bov, biv, evv, xa, xb, os, rc, sem):
    copies = [
        pltpu.make_async_copy(a, b, sem.at[i])
        for i, (a, b) in enumerate(((bo_hbm, bov), (bi_hbm, biv), (ev_hbm, evv), (q_hbm, qv)))
    ]
    for c in copies:
        c.start()
    for c in copies:
        c.wait()
    for t in range(32):
        rc[t:t + 1, :] = evv[0:1, t * 128:t * 128 + 128]
    rec = 1.0 / (rc[...] + damping)
    left_in, left_out = row_maps(bov[0])
    first, last = col_maps(biv[0])

    def get(t):
        return qv[0, :, t * 128:t * 128 + 128]

    def put(t, v):
        o_ref[:, t * 128:t * 128 + 128] = v.astype(BF16)

    prep_body(nq, get, put, left_in, left_out, first, last, rec, xa, xb, os, group)


def prep(q, bo, bi, ev):
    nq = q.shape[1]
    group = 16 if nq % 16 == 0 else nq
    return pl.pallas_call(
        functools.partial(prep_kernel, nq, group),
        out_shape=jax.ShapeDtypeStruct(q.shape[1:], BF16),
        in_specs=[pl.BlockSpec(memory_space=pltpu.HBM)] * 4,
        out_specs=pl.BlockSpec(memory_space=pltpu.VMEM),
        scratch_shapes=[
            pltpu.VMEM(q.shape, BF16),
            pltpu.VMEM(bo.shape, F32),
            pltpu.VMEM(bi.shape, F32),
            pltpu.VMEM(ev.shape, F32),
            pltpu.VMEM((32 * nq, 128), F32),
            pltpu.VMEM((32 * nq, 128), F32),
            pltpu.VMEM((32 * nq, 128), F32),
            pltpu.VMEM((32, 128), F32),
            pltpu.SemaphoreType.DMA((4,)),
        ],
        compiler_params=pltpu.CompilerParams(vmem_limit_bytes=24 << 20),
    )(q, bo, bi, ev)


PIECES = 4


def score_kernel(train_hbm, own, near, mid, mid2, far, far2, mine, core, across, both, tv, qv, pv, sem):
    n = tv.shape[0]
    step = n // PIECES
    copies = [
        pltpu.make_async_copy(train_hbm.at[0, pl.ds(i * step, step)], tv.at[pl.ds(i * step, step)], sem.at[i])
        for i in range(PIECES)
    ]
    for c in copies:
        c.start()
    half = 16 * lax.axis_index("grp")
    rest = 16 - half
    rows = own.shape[0]
    slot = lax.axis_index("ex") ^ lax.axis_index("lyr")

    def at(m, extra):
        return pl.ds(pl.multiple_of((slot ^ m) * rows + extra, 16), 16)

    whole = lambda m: pl.ds(pl.multiple_of((slot ^ m) * rows, 16), rows)
    qv[whole(0), :] = own[...]
    qv[whole(1), :] = near[...]
    qv[at(2, half), :] = mid[...]
    qv[at(2, rest), :] = mid2[...]
    qv[at(3, half), :] = far[...]
    qv[at(3, rest), :] = far2[...]
    for i, c in enumerate(copies):
        c.wait()
        part = dot(tv[i * step:i * step + step, :], qv[...], 1, 1)
        pv[:, i * step:i * step + step] = part.T * (1.0 / math.sqrt(GR * GC))
    for m, o in enumerate((mine, core, across, both)):
        o[...] = pv[m * rows:m * rows + rows, :]


def score(train, *chunks):
    n, f = train.shape[1:]
    rows = chunks[0].shape[0]
    return pl.pallas_call(
        score_kernel,
        out_shape=[jax.ShapeDtypeStruct((rows, n), F32)] * 4,
        in_specs=[pl.BlockSpec(memory_space=pltpu.HBM)] + [pl.BlockSpec(memory_space=pltpu.VMEM)] * 6,
        out_specs=[pl.BlockSpec(memory_space=pltpu.VMEM)] * 4,
        scratch_shapes=[
            pltpu.VMEM((n, f), BF16),
            pltpu.VMEM((4 * rows, f), BF16),
            pltpu.VMEM((4 * rows, n), F32),
            pltpu.SemaphoreType.DMA((PIECES,)),
        ],
        compiler_params=pltpu.CompilerParams(vmem_limit_bytes=32 << 20),
    )(train, *chunks)


def flip(x, axis, mask, size):
    return lax.ppermute(x, axis, [(i, i ^ mask) for i in range(size)])


def local(sizes, train, query, bo, bi, ev):
    ready = prep(query, bo, bi, ev)
    ex, lyr, grp = sizes
    if (ex, lyr, grp) != (4, 4, 2) or ready.shape[0] != 32:
        everyone = lax.all_gather(ready, "ex", axis=0, tiled=True)
        part = dot(train[0], everyone, 1, 1)
        return lax.psum_scatter(part, "lyr", scatter_dimension=1, tiled=True) / math.sqrt(GR * GC)
    start = 16 * lax.axis_index("grp")
    half = lax.dynamic_slice_in_dim(ready, start, 16, 0)
    mid = flip(half, "ex", 2, 4)
    far = flip(half, "ex", 3, 4)
    near = flip(ready, "ex", 1, 4)
    mid2 = flip(mid, "grp", 1, 2)
    far2 = flip(far, "grp", 1, 2)
    mine, core, across, both = score(train, ready, near, mid, mid2, far, far2)
    total = mine + flip(core, "lyr", 1, 4) + flip(across, "lyr", 2, 4) + flip(both, "lyr", 3, 4)
    return total.T


def solution(mesh):
    sizes = tuple(mesh.shape[a] for a in ("ex", "lyr", "grp"))
    return jax.shard_map(
        functools.partial(local, sizes),
        mesh=mesh,
        in_specs=(
            P("lyr", ("grp", "ex"), None),
            P("lyr", "ex", None),
            P("lyr", None, None),
            P("lyr", None, None),
            P("lyr", None),
        ),
        out_specs=P(("grp", "ex"), "lyr"),
        check_vma=False,
    )
```

```python
import functools
import math

import jax, jax.numpy as jnp
from jax import lax
from jax.experimental import pallas as pl
from jax.experimental.pallas import tpu as pltpu
from jax.sharding import PartitionSpec as P

GR = 64
GC = 64
damping = 0.1
F32, BF16 = jnp.float32, jnp.bfloat16
VM = pl.BlockSpec(memory_space=pltpu.VMEM)
HB = pl.BlockSpec(memory_space=pl.ANY)


def dot(a, b, ca=1, cb=0):
    return lax.dot_general(a, b, (((ca,), (cb,)), ((), ())), preferred_element_type=F32)
def split(x):
    h = x.astype(BF16)
    return h, (x - h.astype(F32)).astype(BF16)
def selector(rows, which, swap):
    k = lax.broadcasted_iota(jnp.int32, (rows, 64), 0)
    b = lax.broadcasted_iota(jnp.int32, (rows, 64), 1)
    kk = k % 64
    par = kk // 32
    if swap: par = 1 - par
    hit = b == 2 * (kk % 32) + par
    if which == 1: hit = hit & (k < 128)
    if which == 2: hit = hit & (k >= 128)
    return jnp.where(hit, 1.0, 0.0).astype(BF16)
def row_maps(bo):
    h, l = split(bo)
    sel = selector(64, 0, False)
    outs = []
    for cb in (1, 0):
        th, tl = dot(sel, h, 1, cb).astype(BF16), dot(sel, l, 1, cb).astype(BF16)
        parts = []
        for swap in (False, True):
            full = dot(th, selector(192, 1, swap), 1, 1) + dot(tl, selector(192, 2, swap), 1, 1)
            parts.append(full[32 * swap:32 * swap + 32])
        outs.append(jnp.concatenate(parts, 0).astype(BF16))
    return outs
def col_maps(bi):
    h, l = split(bi)
    r = lax.broadcasted_iota(jnp.int32, (128, 64), 0) % 64
    c = lax.broadcasted_iota(jnp.int32, (128, 64), 1)
    e = jnp.where(r == c, 1.0, 0.0).astype(BF16)
    i = lax.broadcasted_iota(jnp.int32, (128, 128), 0) // 64
    j = lax.broadcasted_iota(jnp.int32, (128, 128), 1) // 64
    same = i == j
    def tile(x, cb):
        t = dot(e, x, 1, cb).astype(BF16)
        return dot(t, e, 1, 1)
    def pick(t, m): return jnp.where(m, t, 0.0).astype(BF16)
    th, tl = tile(h, 0), tile(l, 0)
    diff = jnp.logical_not(same)
    first = jnp.concatenate([jnp.concatenate([pick(th, same), pick(th, diff)], 1), jnp.concatenate([pick(tl, same), pick(tl, diff)], 1)], 0)
    uh, ul = tile(h, 1), tile(l, 1)
    last = jnp.concatenate([pick(uh, same), pick(uh, same), pick(ul, same)], 0)
    return first, last
def prep_body(nq, get, put, left_in, left_out, first, last, rec, xa, xb, os, group=8):
    g = jnp.concatenate([get(t) for t in range(32)], 0)
    x = dot(jnp.concatenate([g, g], 1), first)
    xa[...] = x[:, :128]
    xb[...] = x[:, 128:]
    lane = lax.broadcasted_iota(jnp.int32, (32, 128), 1) < 64
    for q0 in range(0, nq, group):
        qs = range(q0, q0 + group)
        ww = jnp.concatenate([jnp.concatenate([r[pl.ds(q, 32, stride=nq), :] for q in qs], 1) for r in (xa, xb)], 0)
        h, l = split(ww)
        r = dot(left_in, jnp.concatenate([h, l, h], 0))
        ys, yr = [], []
        for i in range(group):
            s = slice(i * 128, i * 128 + 128)
            y = jnp.where(lane, r[:32, s], r[32:, s]) * rec
            ys.append(y); yr.append(pltpu.roll(y, 64, 1))
        yy = jnp.concatenate([jnp.concatenate(ys, 1), jnp.concatenate(yr, 1)], 0)
        h, l = split(yy)
        r = dot(left_out, jnp.concatenate([h, l, h], 0))
        z = jnp.concatenate([jnp.where(lane, r[:32, i * 128:i * 128 + 128], r[32:, i * 128:i * 128 + 128]) for i in range(group)], 0)
        h, l = split(z)
        os[pl.ds(q0 * 32, group * 32), :] = dot(jnp.concatenate([h, l, h], 1), last)
    for t in range(32):
        put(t, os[pl.ds(t, nq, stride=32), :])

def scores_of(train, ready):
    return dot(train, ready, 1, 1).T * (1.0 / math.sqrt(GR * GC))


def first_kernel(nq, q_hbm, bo_hbm, bi_hbm, ev_hbm, train_hbm, tv, lin, lout, fst, lst, rec, part, qv, bov, biv, evv, xa, xb, os, pv, sem):
    copies = [
        pltpu.make_async_copy(a, b, sem.at[i])
        for i, (a, b) in enumerate(((bo_hbm, bov), (bi_hbm, biv), (ev_hbm, evv), (q_hbm, qv), (train_hbm.at[0], tv)))
    ]
    for c in copies:
        c.start()
    for c in copies[:4]:
        c.wait()
    for t in range(32):
        rec[t:t + 1, :] = 1.0 / (evv[0:1, t * 128:t * 128 + 128] + damping)
    lin[...], lout[...] = row_maps(bov[0])
    fst[...], lst[...] = col_maps(biv[0])

    def put(t, v):
        pv[:, t * 128:t * 128 + 128] = v.astype(BF16)

    prep_body(nq, lambda t: qv[0, :, t * 128:t * 128 + 128], put, lin[...], lout[...], fst[...], lst[...], rec[...], xa, xb, os, 16)
    copies[4].wait()
    part[...] = scores_of(tv[...], pv[...])


def maps_shapes():
    return [
        jax.ShapeDtypeStruct((64, 192), BF16),
        jax.ShapeDtypeStruct((64, 192), BF16),
        jax.ShapeDtypeStruct((256, 256), BF16),
        jax.ShapeDtypeStruct((384, 128), BF16),
        jax.ShapeDtypeStruct((32, 128), F32),
    ]


def work(nq):
    return [pltpu.VMEM((32 * nq, 128), F32)] * 3 + [pltpu.VMEM((nq, GR * GC), BF16)]


def cost(nq, n):
    return pl.CostEstimate(flops=2 * n * 4096 * 2048, bytes_accessed=8 << 20, transcendentals=0)


def first(q, bo, bi, ev, train):
    nq = q.shape[1]
    n, f = train.shape[1:]
    return pl.pallas_call(
        functools.partial(first_kernel, nq),
        out_shape=[jax.ShapeDtypeStruct((n, f), BF16)] + maps_shapes() + [jax.ShapeDtypeStruct((nq, n), F32)],
        in_specs=[HB] * 5,
        out_specs=[VM] * 7,
        scratch_shapes=[
            pltpu.VMEM(q.shape, BF16),
            pltpu.VMEM(bo.shape, F32),
            pltpu.VMEM(bi.shape, F32),
            pltpu.VMEM(ev.shape, F32),
        ] + work(nq) + [pltpu.SemaphoreType.DMA((5,))],
        compiler_params=pltpu.CompilerParams(vmem_limit_bytes=20 << 20),
        cost_estimate=cost(nq, n),
    )(q, bo, bi, ev, train)


def next_kernel(counts, *refs):
    k = len(counts)
    chunks, (tv, lin, lout, fst, lst, rec), part, (xa, xb, os, pv) = refs[:k], refs[k:k + 6], refs[k + 6], refs[k + 7:]
    nq = sum(counts)

    def get(t):
        return jnp.concatenate([c[:, t * 128:t * 128 + 128] for c in chunks], 0)

    def put(t, v):
        pv[:, t * 128:t * 128 + 128] = v.astype(BF16)

    prep_body(nq, get, put, lin[...], lout[...], fst[...], lst[...], rec[...], xa, xb, os, 16)
    part[...] = scores_of(tv[...], pv[...])


def following(chunks, tv, maps):
    counts = [c.shape[0] for c in chunks]
    nq, n = sum(counts), tv.shape[0]
    return pl.pallas_call(
        functools.partial(next_kernel, counts),
        out_shape=jax.ShapeDtypeStruct((nq, n), F32),
        in_specs=[VM] * (len(chunks) + 6),
        out_specs=VM,
        scratch_shapes=work(nq),
        compiler_params=pltpu.CompilerParams(vmem_limit_bytes=20 << 20),
        cost_estimate=cost(nq, n),
    )(*chunks, tv, *maps)


def last_kernel(chunk, tv, lin, lout, fst, lst, rec, p_own, p_near, p_mid, p_rest, mine, core, across, both, xa, xb, os, pv, sv):
    half = 16 * lax.axis_index("grp")
    other = 16 - half
    rows = p_own.shape[0]
    slot = lax.axis_index("ex") ^ lax.axis_index("lyr")

    def at(m, extra, size):
        return pl.ds(pl.multiple_of((slot ^ m) * rows + extra, 16), size)

    sv[at(0, 0, rows), :] = p_own[...]
    sv[at(1, 0, rows), :] = p_near[...]
    sv[at(2, half, 16), :] = p_mid[...]
    sv[at(2, other, 16), :] = p_rest[0:16, :]
    sv[at(3, half, 16), :] = p_rest[16:32, :]

    def put(t, v):
        pv[:, t * 128:t * 128 + 128] = v.astype(BF16)

    prep_body(16, lambda t: chunk[:, t * 128:t * 128 + 128], put, lin[...], lout[...], fst[...], lst[...], rec[...], xa, xb, os, 16)
    sv[at(3, other, 16), :] = scores_of(tv[...], pv[...])
    for m, o in enumerate((mine, core, across, both)):
        o[...] = sv[m * rows:m * rows + rows, :].astype(o.dtype)


def final(chunk, tv, maps, *parts):
    rows, n = parts[0].shape
    return pl.pallas_call(
        last_kernel,
        out_shape=[jax.ShapeDtypeStruct((rows, n), d) for d in (F32, F32, SENT, SENT)],
        in_specs=[VM] * (7 + len(parts)),
        out_specs=[VM] * 4,
        scratch_shapes=work(16) + [pltpu.VMEM((4 * rows, n), F32)],
        compiler_params=pltpu.CompilerParams(vmem_limit_bytes=20 << 20),
        cost_estimate=cost(16, n),
    )(chunk, tv, *maps, *parts)


SENT = BF16


def flip(x, axis, mask, size):
    return lax.ppermute(x, axis, [(i, i ^ mask) for i in range(size)])


def plain(sizes, train, query, bo, bi, ev):
    g = query.shape[1]
    matrix = query[0].astype(F32).reshape(g, GR, GC)
    high = lax.Precision.HIGHEST
    x = jnp.einsum("ba,qbc->qac", bo[0], matrix, precision=high)
    x = jnp.einsum("qac,cd->qad", x, bi[0], precision=high)
    x = x / (ev.reshape(1, GR, GC) + damping)
    x = jnp.einsum("ab,qbc->qac", bo[0], x, precision=high)
    x = jnp.einsum("qac,dc->qad", x, bi[0], precision=high)
    ready = lax.all_gather(x.reshape(g, GR * GC).astype(BF16), "ex", axis=0, tiled=True)
    part = dot(train[0], ready, 1, 1)
    return lax.psum_scatter(part, "lyr", scatter_dimension=1, tiled=True) / math.sqrt(GR * GC)


def local(sizes, train, query, bo, bi, ev):
    if sizes != (4, 4, 2) or query.shape[1] != 32:
        return plain(sizes, train, query, bo, bi, ev)
    raw = query[0]
    start = 16 * lax.axis_index("grp")
    half = lax.dynamic_slice_in_dim(raw, start, 16, 0)
    mid = flip(half, "ex", 2, 4)
    far = flip(half, "ex", 3, 4)
    near = flip(raw, "ex", 1, 4)
    tv, *rest = first(query, bo, bi, ev, train)
    maps, p_own = rest[:5], rest[5]
    mid2 = flip(mid, "grp", 1, 2)
    far2 = flip(far, "grp", 1, 2)
    p_near = following([near], tv, maps)
    p_mid = following([mid], tv, maps)
    p_rest = following([mid2, far], tv, maps)
    mine, core, across, both = final(far2, tv, maps, p_own, p_near, p_mid, p_rest)
    total = mine + flip(core, "lyr", 1, 4)
    total = total + flip(across, "lyr", 2, 4).astype(F32) + flip(both, "lyr", 3, 4).astype(F32)
    return total.T


def solution(mesh):
    sizes = tuple(mesh.shape[a] for a in ("ex", "lyr", "grp"))
    return jax.shard_map(
        functools.partial(local, sizes),
        mesh=mesh,
        in_specs=(
            P("lyr", ("grp", "ex"), None),
            P("lyr", "ex", None),
            P("lyr", None, None),
            P("lyr", None, None),
            P("lyr", None),
        ),
        out_specs=P(("grp", "ex"), "lyr"),
        check_vma=False,
    )
```

```python
import functools
import math

import jax, jax.numpy as jnp
from jax import lax
from jax.experimental import pallas as pl
from jax.experimental.pallas import tpu as pltpu
from jax.sharding import PartitionSpec as P

GR = 64
GC = 64
damping = 0.1
F32, BF16 = jnp.float32, jnp.bfloat16
VM = pl.BlockSpec(memory_space=pltpu.VMEM)


def dot(a, b, ca=1, cb=0):
    return lax.dot_general(a, b, (((ca,), (cb,)), ((), ())), preferred_element_type=F32)
def split(x):
    h = x.astype(BF16)
    return h, (x - h.astype(F32)).astype(BF16)
def selector(rows, which, swap):
    k = lax.broadcasted_iota(jnp.int32, (rows, 64), 0)
    b = lax.broadcasted_iota(jnp.int32, (rows, 64), 1)
    kk = k % 64
    par = kk // 32
    if swap: par = 1 - par
    hit = b == 2 * (kk % 32) + par
    if which == 1: hit = hit & (k < 128)
    if which == 2: hit = hit & (k >= 128)
    return jnp.where(hit, 1.0, 0.0).astype(BF16)
def row_maps(bo):
    h, l = split(bo)
    sel = selector(64, 0, False)
    outs = []
    for cb in (1, 0):
        th, tl = dot(sel, h, 1, cb).astype(BF16), dot(sel, l, 1, cb).astype(BF16)
        parts = []
        for swap in (False, True):
            full = dot(th, selector(192, 1, swap), 1, 1) + dot(tl, selector(192, 2, swap), 1, 1)
            parts.append(full[32 * swap:32 * swap + 32])
        outs.append(jnp.concatenate(parts, 0).astype(BF16))
    return outs
def col_maps(bi):
    h, l = split(bi)
    r = lax.broadcasted_iota(jnp.int32, (128, 64), 0) % 64
    c = lax.broadcasted_iota(jnp.int32, (128, 64), 1)
    e = jnp.where(r == c, 1.0, 0.0).astype(BF16)
    i = lax.broadcasted_iota(jnp.int32, (128, 128), 0) // 64
    j = lax.broadcasted_iota(jnp.int32, (128, 128), 1) // 64
    same = i == j
    def tile(x, cb):
        t = dot(e, x, 1, cb).astype(BF16)
        return dot(t, e, 1, 1)
    def pick(t, m): return jnp.where(m, t, 0.0).astype(BF16)
    th, tl = tile(h, 0), tile(l, 0)
    diff = jnp.logical_not(same)
    first = jnp.concatenate([jnp.concatenate([pick(th, same), pick(th, diff)], 1), jnp.concatenate([pick(tl, same), pick(tl, diff)], 1)], 0)
    uh, ul = tile(h, 1), tile(l, 1)
    last = jnp.concatenate([pick(uh, same), pick(uh, same), pick(ul, same)], 0)
    return first, last
def prep_body(nq, get, put, left_in, left_out, first, last, rec, xa, xb, os, group=8):
    g = jnp.concatenate([get(t) for t in range(32)], 0)
    x = dot(jnp.concatenate([g, g], 1), first)
    xa[...] = x[:, :128]
    xb[...] = x[:, 128:]
    lane = lax.broadcasted_iota(jnp.int32, (32, 128), 1) < 64
    for q0 in range(0, nq, group):
        qs = range(q0, q0 + group)
        ww = jnp.concatenate([jnp.concatenate([r[pl.ds(q, 32, stride=nq), :] for q in qs], 1) for r in (xa, xb)], 0)
        h, l = split(ww)
        r = dot(left_in, jnp.concatenate([h, l, h], 0))
        ys, yr = [], []
        for i in range(group):
            s = slice(i * 128, i * 128 + 128)
            y = jnp.where(lane, r[:32, s], r[32:, s]) * rec
            ys.append(y); yr.append(pltpu.roll(y, 64, 1))
        yy = jnp.concatenate([jnp.concatenate(ys, 1), jnp.concatenate(yr, 1)], 0)
        h, l = split(yy)
        r = dot(left_out, jnp.concatenate([h, l, h], 0))
        z = jnp.concatenate([jnp.where(lane, r[:32, i * 128:i * 128 + 128], r[32:, i * 128:i * 128 + 128]) for i in range(group)], 0)
        h, l = split(z)
        os[pl.ds(q0 * 32, group * 32), :] = dot(jnp.concatenate([h, l, h], 1), last)
    for t in range(32):
        put(t, os[pl.ds(t, nq, stride=32), :])

def scores_of(train, ready):
    return dot(train, ready, 1, 1).T * (1.0 / math.sqrt(GR * GC))


def first_kernel(nq, q_hbm, bo_hbm, bi_hbm, ev_hbm, train_hbm, tv, lin, lout, fst, lst, rec, out, qv, bov, biv, evv, xa, xb, os, sem):
    copies = [
        pltpu.make_async_copy(a, b, sem.at[i])
        for i, (a, b) in enumerate(((bo_hbm, bov), (bi_hbm, biv), (ev_hbm, evv), (q_hbm, qv), (train_hbm.at[0], tv)))
    ]
    for c in copies:
        c.start()
    for c in copies[:4]:
        c.wait()
    for t in range(32):
        rec[t:t + 1, :] = 1.0 / (evv[0:1, t * 128:t * 128 + 128] + damping)
    lin[...], lout[...] = row_maps(bov[0])
    fst[...], lst[...] = col_maps(biv[0])

    def put(t, v):
        out[:, t * 128:t * 128 + 128] = v.astype(BF16)

    prep_body(nq, lambda t: qv[0, :, t * 128:t * 128 + 128], put, lin[...], lout[...], fst[...], lst[...], rec[...], xa, xb, os, 16)
    copies[4].wait()


def maps_shapes():
    return [
        jax.ShapeDtypeStruct((64, 192), BF16),
        jax.ShapeDtypeStruct((64, 192), BF16),
        jax.ShapeDtypeStruct((256, 256), BF16),
        jax.ShapeDtypeStruct((384, 128), BF16),
        jax.ShapeDtypeStruct((32, 128), F32),
    ]


def work(nq):
    return [pltpu.VMEM((32 * nq, 128), F32)] * 3


def settings(us):
    return dict(
        compiler_params=pltpu.CompilerParams(vmem_limit_bytes=20 << 20),
        cost_estimate=pl.CostEstimate(flops=int(us * 1e9), bytes_accessed=int(us * 3.6e6), transcendentals=0),
    )


def first(*args):
    q, bo, bi, ev, train = args
    nq = q.shape[1]
    n, f = train.shape[1:]
    return pl.pallas_call(
        functools.partial(first_kernel, nq),
        out_shape=[jax.ShapeDtypeStruct((n, f), BF16)] + maps_shapes() + [jax.ShapeDtypeStruct((nq, f), BF16)],
        in_specs=[pl.BlockSpec(memory_space=pltpu.HBM)] * 5,
        out_specs=[VM] * 7,
        scratch_shapes=[
            pltpu.VMEM(q.shape, BF16),
            pltpu.VMEM(bo.shape, F32),
            pltpu.VMEM(bi.shape, F32),
            pltpu.VMEM(ev.shape, F32),
        ] + work(nq) + [pltpu.SemaphoreType.DMA((5,))],
        **settings(4),
    )(*(pltpu.with_memory_space_constraint(x, pltpu.HBM) for x in args))


def next_kernel(nq, chunk, lin, lout, fst, lst, rec, out, xa, xb, os):
    def put(t, v):
        out[:, t * 128:t * 128 + 128] = v.astype(BF16)

    prep_body(nq, lambda t: chunk[:, t * 128:t * 128 + 128], put, lin[...], lout[...], fst[...], lst[...], rec[...], xa, xb, os, 16)


def following(chunk, maps):
    nq = chunk.shape[0]
    return pl.pallas_call(
        functools.partial(next_kernel, nq),
        out_shape=jax.ShapeDtypeStruct(chunk.shape, BF16),
        in_specs=[VM] * 6,
        out_specs=VM,
        scratch_shapes=work(nq),
        **settings(nq / 12),
    )(chunk, *maps)


def bulk_kernel(mid2, far, tv, lin, lout, fst, lst, rec, own, near, mid, part, xa, xb, os, pv):
    rows = own.shape[0]
    pv[0:rows, :] = own[...]
    pv[rows:2 * rows, :] = near[...]
    pv[2 * rows:2 * rows + 16, :] = mid[...]

    def get(t):
        s = slice(t * 128, t * 128 + 128)
        return jnp.concatenate([mid2[:, s], far[:, s]], 0)

    def put(t, v):
        pv[2 * rows + 16:, t * 128:t * 128 + 128] = v.astype(BF16)

    prep_body(32, get, put, lin[...], lout[...], fst[...], lst[...], rec[...], xa, xb, os, 16)
    part[...] = scores_of(tv[...], pv[...])


def bulk(mid2, far, tv, maps, own, near, mid):
    rows, f = own.shape
    n = tv.shape[0]
    return pl.pallas_call(
        bulk_kernel,
        out_shape=jax.ShapeDtypeStruct((2 * rows + 48, n), F32),
        in_specs=[VM] * 11,
        out_specs=VM,
        scratch_shapes=work(32) + [pltpu.VMEM((2 * rows + 48, f), BF16)],
        **settings(3.5),
    )(mid2, far, tv, *maps, own, near, mid)


def last_kernel(chunk, tv, lin, lout, fst, lst, rec, part, mine, core, across, both, xa, xb, os, pv, sv):
    half = 16 * lax.axis_index("grp")
    other = 16 - half
    rows = mine.shape[0]
    slot = lax.axis_index("ex") ^ lax.axis_index("lyr")

    def at(m, extra, size):
        return pl.ds(pl.multiple_of((slot ^ m) * rows + extra, 16), size)

    sv[at(0, 0, rows), :] = part[0:rows, :]
    sv[at(1, 0, rows), :] = part[rows:2 * rows, :]
    sv[at(2, half, 16), :] = part[2 * rows:2 * rows + 16, :]
    sv[at(2, other, 16), :] = part[2 * rows + 16:2 * rows + 32, :]
    sv[at(3, half, 16), :] = part[2 * rows + 32:, :]

    def put(t, v):
        pv[:, t * 128:t * 128 + 128] = v.astype(BF16)

    prep_body(16, lambda t: chunk[:, t * 128:t * 128 + 128], put, lin[...], lout[...], fst[...], lst[...], rec[...], xa, xb, os, 16)
    sv[at(3, other, 16), :] = scores_of(tv[...], pv[...])
    for m, o in enumerate((mine, core, across, both)):
        o[...] = sv[m * rows:m * rows + rows, :].astype(o.dtype)


def final(chunk, tv, maps, part, rows):
    n, f = tv.shape
    return pl.pallas_call(
        last_kernel,
        out_shape=[jax.ShapeDtypeStruct((rows, n), d) for d in (F32, F32, SENT, SENT)],
        in_specs=[VM] * 8,
        out_specs=[VM] * 4,
        scratch_shapes=work(16) + [pltpu.VMEM((16, f), BF16), pltpu.VMEM((4 * rows, n), F32)],
        **settings(2),
    )(chunk, tv, *maps, part)


SENT = BF16


def flip(x, axis, mask, size):
    return lax.ppermute(x, axis, [(i, i ^ mask) for i in range(size)])


def plain(sizes, train, query, bo, bi, ev):
    g = query.shape[1]
    matrix = query[0].astype(F32).reshape(g, GR, GC)
    high = lax.Precision.HIGHEST
    x = jnp.einsum("ba,qbc->qac", bo[0], matrix, precision=high)
    x = jnp.einsum("qac,cd->qad", x, bi[0], precision=high)
    x = x / (ev.reshape(1, GR, GC) + damping)
    x = jnp.einsum("ab,qbc->qac", bo[0], x, precision=high)
    x = jnp.einsum("qac,dc->qad", x, bi[0], precision=high)
    ready = lax.all_gather(x.reshape(g, GR * GC).astype(BF16), "ex", axis=0, tiled=True)
    part = dot(train[0], ready, 1, 1)
    return lax.psum_scatter(part, "lyr", scatter_dimension=1, tiled=True) / math.sqrt(GR * GC)


def local(sizes, train, query, bo, bi, ev):
    if sizes != (4, 4, 2) or query.shape[1] != 32:
        return plain(sizes, train, query, bo, bi, ev)
    raw = query[0]
    start = 16 * lax.axis_index("grp")
    half = lax.dynamic_slice_in_dim(raw, start, 16, 0)
    mid = flip(half, "ex", 2, 4)
    far = flip(half, "ex", 3, 4)
    near = flip(raw, "ex", 1, 4)
    tv, *rest = first(query, bo, bi, ev, train)
    maps, own = rest[:5], rest[5]
    near = following(near, maps)
    mid, near = lax.optimization_barrier((mid, near))
    mid2 = flip(mid, "grp", 1, 2)
    mid = following(mid, maps)
    far, mid = lax.optimization_barrier((far, mid))
    far2 = flip(far, "grp", 1, 2)
    part = bulk(mid2, far, tv, maps, own, near, mid)
    mine, core, across, both = final(far2, tv, maps, part, own.shape[0])
    total = mine + flip(core, "lyr", 1, 4)
    total = total + flip(across, "lyr", 2, 4).astype(F32) + flip(both, "lyr", 3, 4).astype(F32)
    return total.T


def solution(mesh):
    sizes = tuple(mesh.shape[a] for a in ("ex", "lyr", "grp"))
    return jax.shard_map(
        functools.partial(local, sizes),
        mesh=mesh,
        in_specs=(
            P("lyr", ("grp", "ex"), None),
            P("lyr", "ex", None),
            P("lyr", None, None),
            P("lyr", None, None),
            P("lyr", None),
        ),
        out_specs=P(("grp", "ex"), "lyr"),
        check_vma=False,
    )
```

```python
import functools
import math

import jax, jax.numpy as jnp
from jax import lax
from jax.experimental import pallas as pl
from jax.experimental.pallas import tpu as pltpu
from jax.sharding import PartitionSpec as P

GR = 64
GC = 64
damping = 0.1
F32, BF16 = jnp.float32, jnp.bfloat16
VM = pl.BlockSpec(memory_space=pltpu.VMEM)


def dot(a, b, ca=1, cb=0):
    return lax.dot_general(a, b, (((ca,), (cb,)), ((), ())), preferred_element_type=F32)
def split(x):
    h = x.astype(BF16)
    return h, (x - h.astype(F32)).astype(BF16)
def selector(rows, which, swap):
    k = lax.broadcasted_iota(jnp.int32, (rows, 64), 0)
    b = lax.broadcasted_iota(jnp.int32, (rows, 64), 1)
    kk = k % 64
    par = kk // 32
    if swap: par = 1 - par
    hit = b == 2 * (kk % 32) + par
    if which == 1: hit = hit & (k < 128)
    if which == 2: hit = hit & (k >= 128)
    return jnp.where(hit, 1.0, 0.0).astype(BF16)
def row_maps(bo):
    h, l = split(bo)
    sel = selector(64, 0, False)
    outs = []
    for cb in (1, 0):
        th, tl = dot(sel, h, 1, cb).astype(BF16), dot(sel, l, 1, cb).astype(BF16)
        parts = []
        for swap in (False, True):
            full = dot(th, selector(192, 1, swap), 1, 1) + dot(tl, selector(192, 2, swap), 1, 1)
            parts.append(full[32 * swap:32 * swap + 32])
        outs.append(jnp.concatenate(parts, 0).astype(BF16))
    return outs
def col_maps(bi):
    h, l = split(bi)
    r = lax.broadcasted_iota(jnp.int32, (128, 64), 0) % 64
    c = lax.broadcasted_iota(jnp.int32, (128, 64), 1)
    e = jnp.where(r == c, 1.0, 0.0).astype(BF16)
    i = lax.broadcasted_iota(jnp.int32, (128, 128), 0) // 64
    j = lax.broadcasted_iota(jnp.int32, (128, 128), 1) // 64
    same = i == j
    def tile(x, cb):
        t = dot(e, x, 1, cb).astype(BF16)
        return dot(t, e, 1, 1)
    def pick(t, m): return jnp.where(m, t, 0.0).astype(BF16)
    th, tl = tile(h, 0), tile(l, 0)
    diff = jnp.logical_not(same)
    first = jnp.concatenate([jnp.concatenate([pick(th, same), pick(th, diff)], 1), jnp.concatenate([pick(tl, same), pick(tl, diff)], 1)], 0)
    uh, ul = tile(h, 1), tile(l, 1)
    last = jnp.concatenate([pick(uh, same), pick(uh, same), pick(ul, same)], 0)
    return first, last
def prep_body(nq, get, put, left_in, left_out, first, last, rec, xa, xb, os, group=8):
    g = jnp.concatenate([get(t) for t in range(32)], 0)
    x = dot(jnp.concatenate([g, g], 1), first)
    xa[...] = x[:, :128]
    xb[...] = x[:, 128:]
    lane = lax.broadcasted_iota(jnp.int32, (32, 128), 1) < 64
    for q0 in range(0, nq, group):
        qs = range(q0, q0 + group)
        ww = jnp.concatenate([jnp.concatenate([r[pl.ds(q, 32, stride=nq), :] for q in qs], 1) for r in (xa, xb)], 0)
        h, l = split(ww)
        r = dot(left_in, jnp.concatenate([h, l, h], 0))
        ys, yr = [], []
        for i in range(group):
            s = slice(i * 128, i * 128 + 128)
            y = jnp.where(lane, r[:32, s], r[32:, s]) * rec
            ys.append(y); yr.append(pltpu.roll(y, 64, 1))
        yy = jnp.concatenate([jnp.concatenate(ys, 1), jnp.concatenate(yr, 1)], 0)
        h, l = split(yy)
        r = dot(left_out, jnp.concatenate([h, l, h], 0))
        z = jnp.concatenate([jnp.where(lane, r[:32, i * 128:i * 128 + 128], r[32:, i * 128:i * 128 + 128]) for i in range(group)], 0)
        h, l = split(z)
        os[pl.ds(q0 * 32, group * 32), :] = dot(jnp.concatenate([h, l, h], 1), last)
    for t in range(32):
        put(t, os[pl.ds(t, nq, stride=32), :])

def scores_of(train, ready):
    return dot(train, ready, 1, 1).T * (1.0 / math.sqrt(GR * GC))


def first_kernel(nq, q_hbm, bo_hbm, bi_hbm, ev_hbm, train_hbm, tv, lin, lout, fst, lst, rec, out_a, out_b, qv, bov, biv, evv, xa, xb, os, sem):
    copies = [
        pltpu.make_async_copy(a, b, sem.at[i])
        for i, (a, b) in enumerate(((bo_hbm, bov), (bi_hbm, biv), (ev_hbm, evv), (q_hbm, qv), (train_hbm.at[0], tv)))
    ]
    for c in copies:
        c.start()
    for c in copies[:4]:
        c.wait()
    for t in range(32):
        rec[t:t + 1, :] = 1.0 / (evv[0:1, t * 128:t * 128 + 128] + damping)
    lin[...], lout[...] = row_maps(bov[0])
    fst[...], lst[...] = col_maps(biv[0])

    def put(t, v):
        v = v.astype(BF16)
        out_a[:, t * 128:t * 128 + 128] = v[:16]
        out_b[:, t * 128:t * 128 + 128] = v[16:]

    prep_body(nq, lambda t: qv[0, :, t * 128:t * 128 + 128], put, lin[...], lout[...], fst[...], lst[...], rec[...], xa, xb, os, 16)
    copies[4].wait()


def maps_shapes():
    return [
        jax.ShapeDtypeStruct((64, 192), BF16),
        jax.ShapeDtypeStruct((64, 192), BF16),
        jax.ShapeDtypeStruct((256, 256), BF16),
        jax.ShapeDtypeStruct((384, 128), BF16),
        jax.ShapeDtypeStruct((32, 128), F32),
    ]


def work(nq):
    return [pltpu.VMEM((32 * nq, 128), F32)] * 3


def settings(us):
    return dict(
        compiler_params=pltpu.CompilerParams(vmem_limit_bytes=20 << 20),
        cost_estimate=pl.CostEstimate(flops=int(us * 1e9), bytes_accessed=int(us * 3.6e6), transcendentals=0),
    )


def first(*args):
    q, bo, bi, ev, train = args
    nq = q.shape[1]
    n, f = train.shape[1:]
    return pl.pallas_call(
        functools.partial(first_kernel, nq),
        out_shape=[jax.ShapeDtypeStruct((n, f), BF16)] + maps_shapes() + [jax.ShapeDtypeStruct((16, f), BF16)] * 2,
        in_specs=[pl.BlockSpec(memory_space=pltpu.HBM)] * 5,
        out_specs=[VM] * 8,
        scratch_shapes=[
            pltpu.VMEM(q.shape, BF16),
            pltpu.VMEM(bo.shape, F32),
            pltpu.VMEM(bi.shape, F32),
            pltpu.VMEM(ev.shape, F32),
        ] + work(nq) + [pltpu.SemaphoreType.DMA((5,))],
        **settings(4),
    )(*(pltpu.with_memory_space_constraint(x, pltpu.HBM) for x in args))


def next_kernel(nq, chunk, lin, lout, fst, lst, rec, out, xa, xb, os):
    def put(t, v):
        out[:, t * 128:t * 128 + 128] = v.astype(BF16)

    prep_body(nq, lambda t: chunk[:, t * 128:t * 128 + 128], put, lin[...], lout[...], fst[...], lst[...], rec[...], xa, xb, os, 16)


def following(chunk, maps):
    nq = chunk.shape[0]
    return pl.pallas_call(
        functools.partial(next_kernel, nq),
        out_shape=jax.ShapeDtypeStruct(chunk.shape, BF16),
        in_specs=[VM] * 6,
        out_specs=VM,
        scratch_shapes=work(nq),
        **settings(nq / 12),
    )(chunk, *maps)


def bulk_kernel(*refs):
    *pieces, tv, part, pv = refs
    for i, p in enumerate(pieces):
        pv[i * 16:i * 16 + 16, :] = p[...]
    part[...] = scores_of(tv[...], pv[...])


def bulk(tv, *pieces):
    n, f = tv.shape
    rows = 16 * len(pieces)
    return pl.pallas_call(
        bulk_kernel,
        out_shape=jax.ShapeDtypeStruct((rows, n), F32),
        in_specs=[VM] * (len(pieces) + 1),
        out_specs=VM,
        scratch_shapes=[pltpu.VMEM((rows, f), BF16)],
        **settings(1.5),
    )(*pieces, tv)


def last_kernel(far2, tv, part, mine, core, across, both, sv):
    half = 16 * lax.axis_index("grp")
    other = 16 - half
    rows = mine.shape[0]
    slot = lax.axis_index("ex") ^ lax.axis_index("lyr")

    def at(m, extra, size):
        return pl.ds(pl.multiple_of((slot ^ m) * rows + extra, 16), size)

    sv[at(0, 0, rows), :] = part[0:rows, :]
    sv[at(1, 0, rows), :] = part[rows:2 * rows, :]
    sv[at(2, half, 16), :] = part[2 * rows:2 * rows + 16, :]
    sv[at(2, other, 16), :] = part[2 * rows + 16:2 * rows + 32, :]
    sv[at(3, half, 16), :] = part[2 * rows + 32:, :]
    sv[at(3, other, 16), :] = scores_of(tv[...], far2[...])
    for m, o in enumerate((mine, core, across, both)):
        o[...] = sv[m * rows:m * rows + rows, :].astype(o.dtype)


def final(far2, tv, part, rows):
    n, f = tv.shape
    return pl.pallas_call(
        last_kernel,
        out_shape=[jax.ShapeDtypeStruct((rows, n), d) for d in (F32, F32, SENT, SENT)],
        in_specs=[VM] * 3,
        out_specs=[VM] * 4,
        scratch_shapes=[pltpu.VMEM((4 * rows, n), F32)],
        **settings(1.3),
    )(far2, tv, part)


SENT = BF16


def flip(x, axis, mask, size):
    return lax.ppermute(x, axis, [(i, i ^ mask) for i in range(size)])


def plain(sizes, train, query, bo, bi, ev):
    g = query.shape[1]
    matrix = query[0].astype(F32).reshape(g, GR, GC)
    high = lax.Precision.HIGHEST
    x = jnp.einsum("ba,qbc->qac", bo[0], matrix, precision=high)
    x = jnp.einsum("qac,cd->qad", x, bi[0], precision=high)
    x = x / (ev.reshape(1, GR, GC) + damping)
    x = jnp.einsum("ab,qbc->qac", bo[0], x, precision=high)
    x = jnp.einsum("qac,dc->qad", x, bi[0], precision=high)
    ready = lax.all_gather(x.reshape(g, GR * GC).astype(BF16), "ex", axis=0, tiled=True)
    part = dot(train[0], ready, 1, 1)
    return lax.psum_scatter(part, "lyr", scatter_dimension=1, tiled=True) / math.sqrt(GR * GC)


def local(sizes, train, query, bo, bi, ev):
    if sizes != (4, 4, 2) or query.shape[1] != 32:
        return plain(sizes, train, query, bo, bi, ev)
    start = 16 * lax.axis_index("grp")
    half = lax.dynamic_slice_in_dim(query[0], start, 16, 0)
    mid = flip(half, "ex", 2, 4)
    tv, *rest = first(query, bo, bi, ev, train)
    maps, own_a, own_b = rest[:5], rest[5], rest[6]
    near_a = flip(own_a, "ex", 1, 4)
    mid = following(mid, maps)
    far = flip(mid, "ex", 1, 4)
    mid2 = flip(mid, "grp", 1, 2)
    own_b, mid = lax.optimization_barrier((own_b, mid))
    near_b = flip(own_b, "ex", 1, 4)
    far2 = flip(far, "grp", 1, 2)
    part = bulk(tv, own_a, own_b, near_a, near_b, mid, mid2, far)
    mine, core, across, both = final(far2, tv, part, query.shape[1])
    total = mine + flip(core, "lyr", 1, 4)
    total = total + flip(across, "lyr", 2, 4).astype(F32) + flip(both, "lyr", 3, 4).astype(F32)
    return total.T


def solution(mesh):
    sizes = tuple(mesh.shape[a] for a in ("ex", "lyr", "grp"))
    return jax.shard_map(
        functools.partial(local, sizes),
        mesh=mesh,
        in_specs=(
            P("lyr", ("grp", "ex"), None),
            P("lyr", "ex", None),
            P("lyr", None, None),
            P("lyr", None, None),
            P("lyr", None),
        ),
        out_specs=P(("grp", "ex"), "lyr"),
        check_vma=False,
    )
```

```python
import functools
import math

import jax, jax.numpy as jnp
from jax import lax
from jax.experimental import pallas as pl
from jax.experimental.pallas import tpu as pltpu
from jax.sharding import PartitionSpec as P

GR = 64
GC = 64
damping = 0.1
F32, BF16 = jnp.float32, jnp.bfloat16
VM = pl.BlockSpec(memory_space=pltpu.VMEM)


def dot(a, b, ca=1, cb=0):
    return lax.dot_general(a, b, (((ca,), (cb,)), ((), ())), preferred_element_type=F32)
def split(x):
    h = x.astype(BF16)
    return h, (x - h.astype(F32)).astype(BF16)
def selector(rows, which, swap):
    k = lax.broadcasted_iota(jnp.int32, (rows, 64), 0)
    b = lax.broadcasted_iota(jnp.int32, (rows, 64), 1)
    kk = k % 64
    par = kk // 32
    if swap: par = 1 - par
    hit = b == 2 * (kk % 32) + par
    if which == 1: hit = hit & (k < 128)
    if which == 2: hit = hit & (k >= 128)
    return jnp.where(hit, 1.0, 0.0).astype(BF16)
def row_maps(bo):
    h, l = split(bo)
    sel = selector(64, 0, False)
    outs = []
    for cb in (1, 0):
        th, tl = dot(sel, h, 1, cb).astype(BF16), dot(sel, l, 1, cb).astype(BF16)
        parts = []
        for swap in (False, True):
            full = dot(th, selector(192, 1, swap), 1, 1) + dot(tl, selector(192, 2, swap), 1, 1)
            parts.append(full[32 * swap:32 * swap + 32])
        outs.append(jnp.concatenate(parts, 0).astype(BF16))
    return outs
def col_maps(bi):
    h, l = split(bi)
    r = lax.broadcasted_iota(jnp.int32, (128, 64), 0) % 64
    c = lax.broadcasted_iota(jnp.int32, (128, 64), 1)
    e = jnp.where(r == c, 1.0, 0.0).astype(BF16)
    i = lax.broadcasted_iota(jnp.int32, (128, 128), 0) // 64
    j = lax.broadcasted_iota(jnp.int32, (128, 128), 1) // 64
    same = i == j
    def tile(x, cb):
        t = dot(e, x, 1, cb).astype(BF16)
        return dot(t, e, 1, 1)
    def pick(t, m): return jnp.where(m, t, 0.0).astype(BF16)
    th, tl = tile(h, 0), tile(l, 0)
    diff = jnp.logical_not(same)
    first = jnp.concatenate([jnp.concatenate([pick(th, same), pick(th, diff)], 1), jnp.concatenate([pick(tl, same), pick(tl, diff)], 1)], 0)
    uh, ul = tile(h, 1), tile(l, 1)
    last = jnp.concatenate([pick(uh, same), pick(uh, same), pick(ul, same)], 0)
    return first, last
def prep_body(nq, get, put, left_in, left_out, first, last, rec, xa, xb, os, group=8):
    g = jnp.concatenate([get(t) for t in range(32)], 0)
    x = dot(jnp.concatenate([g, g], 1), first)
    xa[...] = x[:, :128]
    xb[...] = x[:, 128:]
    lane = lax.broadcasted_iota(jnp.int32, (32, 128), 1) < 64
    for q0 in range(0, nq, group):
        qs = range(q0, q0 + group)
        ww = jnp.concatenate([jnp.concatenate([r[pl.ds(q, 32, stride=nq), :] for q in qs], 1) for r in (xa, xb)], 0)
        h, l = split(ww)
        r = dot(left_in, jnp.concatenate([h, l, h], 0))
        ys, yr = [], []
        for i in range(group):
            s = slice(i * 128, i * 128 + 128)
            y = jnp.where(lane, r[:32, s], r[32:, s]) * rec
            ys.append(y); yr.append(pltpu.roll(y, 64, 1))
        yy = jnp.concatenate([jnp.concatenate(ys, 1), jnp.concatenate(yr, 1)], 0)
        h, l = split(yy)
        r = dot(left_out, jnp.concatenate([h, l, h], 0))
        z = jnp.concatenate([jnp.where(lane, r[:32, i * 128:i * 128 + 128], r[32:, i * 128:i * 128 + 128]) for i in range(group)], 0)
        h, l = split(z)
        os[pl.ds(q0 * 32, group * 32), :] = dot(jnp.concatenate([h, l, h], 1), last)
    for t in range(32):
        put(t, os[pl.ds(t, nq, stride=32), :])

def scores_of(train, ready):
    return dot(train, ready, 1, 1).T * (1.0 / math.sqrt(GR * GC))


def first_kernel(nq, q_hbm, bo_hbm, bi_hbm, ev_hbm, train_hbm, tv, out, lin, lout, fst, lst, rec, qv, bov, biv, evv, xa, xb, os, sem):
    copies = [
        pltpu.make_async_copy(a, b, sem.at[i])
        for i, (a, b) in enumerate(((bo_hbm, bov), (bi_hbm, biv), (ev_hbm, evv), (q_hbm, qv), (train_hbm.at[0], tv)))
    ]
    for c in copies:
        c.start()
    for c in copies[:4]:
        c.wait()
    for t in range(32):
        rec[t:t + 1, :] = 1.0 / (evv[0:1, t * 128:t * 128 + 128] + damping)
    lin[...], lout[...] = row_maps(bov[0])
    fst[...], lst[...] = col_maps(biv[0])

    def put(t, v):
        out[:, t * 128:t * 128 + 128] = v.astype(BF16)

    prep_body(nq, lambda t: qv[0, :, t * 128:t * 128 + 128], put, lin[...], lout[...], fst[...], lst[...], rec[...], xa, xb, os, 16)
    copies[4].wait()


def maps_shapes():
    return [
        jax.ShapeDtypeStruct((64, 192), BF16),
        jax.ShapeDtypeStruct((64, 192), BF16),
        jax.ShapeDtypeStruct((256, 256), BF16),
        jax.ShapeDtypeStruct((384, 128), BF16),
        jax.ShapeDtypeStruct((32, 128), F32),
    ]


def work(nq):
    return [pltpu.VMEM((32 * nq, 128), F32)] * 3


def settings(us):
    return dict(
        compiler_params=pltpu.CompilerParams(vmem_limit_bytes=20 << 20),
        cost_estimate=pl.CostEstimate(flops=int(us * 1e9), bytes_accessed=int(us * 3.6e6), transcendentals=0),
    )


def first(*args):
    q, bo, bi, ev, train = args
    nq = q.shape[1]
    return pl.pallas_call(
        functools.partial(first_kernel, nq),
        out_shape=[jax.ShapeDtypeStruct(x.shape[1:], BF16) for x in (train, q)] + maps_shapes(),
        in_specs=[pl.BlockSpec(memory_space=pltpu.HBM)] * 5,
        out_specs=[VM] * 7,
        scratch_shapes=[pltpu.VMEM(q.shape, BF16)]
        + [pltpu.VMEM(x.shape, F32) for x in (bo, bi, ev)]
        + work(nq)
        + [pltpu.SemaphoreType.DMA((5,))],
        **settings(4),
    )(*(pltpu.with_memory_space_constraint(x, pltpu.HBM) for x in args))


def next_kernel(nq, chunk, lin, lout, fst, lst, rec, out, xa, xb, os):
    def put(t, v):
        out[:, t * 128:t * 128 + 128] = v.astype(BF16)

    prep_body(nq, lambda t: chunk[:, t * 128:t * 128 + 128], put, lin[...], lout[...], fst[...], lst[...], rec[...], xa, xb, os, 16)


def following(chunk, maps):
    nq = chunk.shape[0]
    return pl.pallas_call(
        functools.partial(next_kernel, nq),
        out_shape=jax.ShapeDtypeStruct(chunk.shape, BF16),
        in_specs=[VM] * 6,
        out_specs=VM,
        scratch_shapes=work(nq),
        **settings(nq / 12),
    )(chunk, *maps)


def bulk_kernel(own, near, mid, tv, lin, lout, fst, lst, rec, part, xa, xb, os, pv):
    rows = own.shape[0]
    pv[0:rows, :] = own[...]
    pv[2 * rows:, :] = mid[...]

    def put(t, v):
        pv[rows:2 * rows, t * 128:t * 128 + 128] = v.astype(BF16)

    prep_body(rows, lambda t: near[:, t * 128:t * 128 + 128], put, lin[...], lout[...], fst[...], lst[...], rec[...], xa, xb, os, 16)
    part[...] = scores_of(tv[...], pv[...])


def bulk(own, near, mid, tv, maps):
    rows, f = own.shape
    n = tv.shape[0]
    return pl.pallas_call(
        bulk_kernel,
        out_shape=jax.ShapeDtypeStruct((2 * rows + 16, n), F32),
        in_specs=[VM] * 9,
        out_specs=VM,
        scratch_shapes=work(rows) + [pltpu.VMEM((2 * rows + 16, f), BF16)],
        **settings(3.5),
    )(own, near, mid, tv, *maps)


def last_kernel(mid2, far, far2, tv, part, mine, core, across, both, pv, sv):
    half = 16 * lax.axis_index("grp")
    other = 16 - half
    rows = mine.shape[0]
    slot = lax.axis_index("ex") ^ lax.axis_index("lyr")

    def at(m, extra, size):
        return pl.ds(pl.multiple_of((slot ^ m) * rows + extra, 16), size)

    sv[at(0, 0, rows), :] = part[0:rows, :]
    sv[at(1, 0, rows), :] = part[rows:2 * rows, :]
    sv[at(3, half, 16), :] = part[2 * rows:, :]
    for i, p in enumerate((mid2, far, far2)):
        pv[i * 16:i * 16 + 16, :] = p[...]
    late = scores_of(tv[...], pv[...])
    sv[at(3, other, 16), :] = late[0:16]
    sv[at(2, half, 16), :] = late[16:32]
    sv[at(2, other, 16), :] = late[32:48]
    for m, o in enumerate((mine, core, across, both)):
        o[...] = sv[m * rows:m * rows + rows, :].astype(o.dtype)


def final(mid2, far, far2, tv, part, rows):
    n, f = tv.shape
    return pl.pallas_call(
        last_kernel,
        out_shape=[jax.ShapeDtypeStruct((rows, n), d) for d in (F32, F32, SENT, SENT)],
        in_specs=[VM] * 5,
        out_specs=[VM] * 4,
        scratch_shapes=[pltpu.VMEM((48, f), BF16), pltpu.VMEM((4 * rows, n), F32)],
        **settings(1.3),
    )(mid2, far, far2, tv, part)


SENT = BF16


def flip(x, axis, mask, size):
    return lax.ppermute(x, axis, [(i, i ^ mask) for i in range(size)])


def plain(sizes, train, query, bo, bi, ev):
    g = query.shape[1]
    matrix = query[0].astype(F32).reshape(g, GR, GC)
    high = lax.Precision.HIGHEST
    x = jnp.einsum("ba,qbc->qac", bo[0], matrix, precision=high)
    x = jnp.einsum("qac,cd->qad", x, bi[0], precision=high)
    x = x / (ev.reshape(1, GR, GC) + damping)
    x = jnp.einsum("ab,qbc->qac", bo[0], x, precision=high)
    x = jnp.einsum("qac,dc->qad", x, bi[0], precision=high)
    ready = lax.all_gather(x.reshape(g, GR * GC).astype(BF16), "ex", axis=0, tiled=True)
    part = dot(train[0], ready, 1, 1)
    return lax.psum_scatter(part, "lyr", scatter_dimension=1, tiled=True) / math.sqrt(GR * GC)


def local(sizes, train, query, bo, bi, ev):
    if sizes != (4, 4, 2) or query.shape[1] != 32:
        return plain(sizes, train, query, bo, bi, ev)
    start = 16 * lax.axis_index("grp")
    half = lax.dynamic_slice_in_dim(query[0], start, 16, 0)
    mid = flip(half, "ex", 3, 4)
    near = flip(query[0], "ex", 1, 4)
    tv, own, *maps = first(query, bo, bi, ev, train)
    mid = following(mid, maps)
    mid2 = flip(mid, "grp", 1, 2)
    far = flip(mid, "ex", 1, 4)
    far2 = lax.ppermute(mid, ("grp", "ex"), [(g * 4 + z, (1 - g) * 4 + (z ^ 1)) for g in range(2) for z in range(4)])
    part = bulk(own, near, mid, tv, maps)
    mine, core, across, both = final(mid2, far, far2, tv, part, query.shape[1])
    total = mine + flip(core, "lyr", 1, 4)
    total = total + flip(across, "lyr", 2, 4).astype(F32) + flip(both, "lyr", 3, 4).astype(F32)
    return total.T


def solution(mesh):
    sizes = tuple(mesh.shape[a] for a in ("ex", "lyr", "grp"))
    return jax.shard_map(
        functools.partial(local, sizes),
        mesh=mesh,
        in_specs=(
            P("lyr", ("grp", "ex"), None),
            P("lyr", "ex", None),
            P("lyr", None, None),
            P("lyr", None, None),
            P("lyr", None),
        ),
        out_specs=P(("grp", "ex"), "lyr"),
        check_vma=False,
    )
```

```python
import functools
import math

import jax, jax.numpy as jnp
from jax import lax
from jax.experimental import pallas as pl
from jax.experimental.pallas import tpu as pltpu
from jax.sharding import PartitionSpec as P

GR = 64
GC = 64
damping = 0.1
F32, BF16 = jnp.float32, jnp.bfloat16
VM = pl.BlockSpec(memory_space=pltpu.VMEM)


def dot(a, b, ca=1, cb=0):
    return lax.dot_general(a, b, (((ca,), (cb,)), ((), ())), preferred_element_type=F32)
def split(x):
    h = x.astype(BF16)
    return h, (x - h.astype(F32)).astype(BF16)
def selector(rows, which, swap):
    k = lax.broadcasted_iota(jnp.int32, (rows, 64), 0)
    b = lax.broadcasted_iota(jnp.int32, (rows, 64), 1)
    kk = k % 64
    par = kk // 32
    if swap: par = 1 - par
    hit = b == 2 * (kk % 32) + par
    if which == 1: hit = hit & (k < 128)
    if which == 2: hit = hit & (k >= 128)
    return jnp.where(hit, 1.0, 0.0).astype(BF16)
def row_maps(bo):
    h, l = split(bo)
    sel = selector(64, 0, False)
    outs = []
    for cb in (1, 0):
        th, tl = dot(sel, h, 1, cb).astype(BF16), dot(sel, l, 1, cb).astype(BF16)
        parts = []
        for swap in (False, True):
            full = dot(th, selector(192, 1, swap), 1, 1) + dot(tl, selector(192, 2, swap), 1, 1)
            parts.append(full[32 * swap:32 * swap + 32])
        outs.append(jnp.concatenate(parts, 0).astype(BF16))
    return outs
def col_maps(bi):
    h, l = split(bi)
    r = lax.broadcasted_iota(jnp.int32, (128, 64), 0) % 64
    c = lax.broadcasted_iota(jnp.int32, (128, 64), 1)
    e = jnp.where(r == c, 1.0, 0.0).astype(BF16)
    i = lax.broadcasted_iota(jnp.int32, (128, 128), 0) // 64
    j = lax.broadcasted_iota(jnp.int32, (128, 128), 1) // 64
    same = i == j
    def tile(x, cb):
        t = dot(e, x, 1, cb).astype(BF16)
        return dot(t, e, 1, 1)
    def pick(t, m): return jnp.where(m, t, 0.0).astype(BF16)
    th, tl = tile(h, 0), tile(l, 0)
    diff = jnp.logical_not(same)
    first = jnp.concatenate([jnp.concatenate([pick(th, same), pick(th, diff)], 1), jnp.concatenate([pick(tl, same), pick(tl, diff)], 1)], 0)
    uh, ul = tile(h, 1), tile(l, 1)
    last = jnp.concatenate([pick(uh, same), pick(uh, same), pick(ul, same)], 0)
    return first, last
def prep_body(nq, get, put, left_in, left_out, first, last, rec, group=16):
    g = jnp.concatenate([get(t) for t in range(32)], 0)
    x = dot(jnp.concatenate([g, g], 1), first)
    both = [jnp.swapaxes(v.reshape(32, nq, 128), 0, 1) for v in (x[:, :128], x[:, 128:])]
    lane = lax.broadcasted_iota(jnp.int32, (32, 128), 1) < 64
    for q0 in range(0, nq, group):
        qs = range(q0, q0 + group)
        ww = jnp.concatenate([jnp.concatenate([r[q] for q in qs], 1) for r in both], 0)
        h, l = split(ww)
        r = dot(left_in, jnp.concatenate([h, l, h], 0))
        ys, yr = [], []
        for i in range(group):
            s = slice(i * 128, i * 128 + 128)
            y = jnp.where(lane, r[:32, s], r[32:, s]) * rec
            ys.append(y); yr.append(pltpu.roll(y, 64, 1))
        yy = jnp.concatenate([jnp.concatenate(ys, 1), jnp.concatenate(yr, 1)], 0)
        h, l = split(yy)
        r = dot(left_out, jnp.concatenate([h, l, h], 0))
        z = jnp.concatenate([jnp.where(lane, r[:32, i * 128:i * 128 + 128], r[32:, i * 128:i * 128 + 128]) for i in range(group)], 0)
        h, l = split(z)
        o = dot(jnp.concatenate([h, l, h], 1), last)
        o = jnp.swapaxes(o.reshape(group, 32, 128), 0, 1)
        for t in range(32):
            put(t, o[t], q0)

def scores_of(train, ready):
    return dot(train, ready, 1, 1).T * (1.0 / math.sqrt(GR * GC))


def first_kernel(nq, q_hbm, bo_hbm, bi_hbm, ev_hbm, train_hbm, tv, out, lin, lout, fst, lst, rec, qv, bov, biv, evv, sem):
    copies = [
        pltpu.make_async_copy(a, b, sem.at[i])
        for i, (a, b) in enumerate(((bo_hbm, bov), (bi_hbm, biv), (ev_hbm, evv), (q_hbm, qv), (train_hbm.at[0], tv)))
    ]
    for c in copies:
        c.start()
    for c in copies[:4]:
        c.wait()
    for t in range(32):
        rec[t:t + 1, :] = 1.0 / (evv[0:1, t * 128:t * 128 + 128] + damping)
    lin[...], lout[...] = row_maps(bov[0])
    fst[...], lst[...] = col_maps(biv[0])

    def put(t, v, at):
        out[at:at + v.shape[0], t * 128:t * 128 + 128] = v.astype(BF16)

    prep_body(nq, lambda t: qv[0, :, t * 128:t * 128 + 128], put, lin[...], lout[...], fst[...], lst[...], rec[...], 16)
    copies[4].wait()


def maps_shapes():
    return [
        jax.ShapeDtypeStruct((64, 192), BF16),
        jax.ShapeDtypeStruct((64, 192), BF16),
        jax.ShapeDtypeStruct((256, 256), BF16),
        jax.ShapeDtypeStruct((384, 128), BF16),
        jax.ShapeDtypeStruct((32, 128), F32),
    ]


def settings(us):
    return dict(
        compiler_params=pltpu.CompilerParams(vmem_limit_bytes=20 << 20),
        cost_estimate=pl.CostEstimate(flops=int(us * 1e9), bytes_accessed=int(us * 3.6e6), transcendentals=0),
    )


def first(*args):
    q, bo, bi, ev, train = args
    nq = q.shape[1]
    return pl.pallas_call(
        functools.partial(first_kernel, nq),
        out_shape=[jax.ShapeDtypeStruct(x.shape[1:], BF16) for x in (train, q)] + maps_shapes(),
        in_specs=[pl.BlockSpec(memory_space=pltpu.HBM)] * 5,
        out_specs=[VM] * 7,
        scratch_shapes=[pltpu.VMEM(q.shape, BF16)]
        + [pltpu.VMEM(x.shape, F32) for x in (bo, bi, ev)]
        + [pltpu.SemaphoreType.DMA((5,))],
        **settings(4),
    )(*(pltpu.with_memory_space_constraint(x, pltpu.HBM) for x in args))


def next_kernel(nq, chunk, lin, lout, fst, lst, rec, out):
    def put(t, v, at):
        out[at:at + v.shape[0], t * 128:t * 128 + 128] = v.astype(BF16)

    prep_body(nq, lambda t: chunk[:, t * 128:t * 128 + 128], put, lin[...], lout[...], fst[...], lst[...], rec[...], 16)


def following(chunk, maps):
    nq = chunk.shape[0]
    return pl.pallas_call(
        functools.partial(next_kernel, nq),
        out_shape=jax.ShapeDtypeStruct(chunk.shape, BF16),
        in_specs=[VM] * 6,
        out_specs=VM,
        **settings(nq / 12),
    )(chunk, *maps)


def bulk_kernel(own, near, mid, tv, lin, lout, fst, lst, rec, part, pv):
    rows = own.shape[0]
    pv[0:rows, :] = own[...]
    pv[2 * rows:, :] = mid[...]

    def put(t, v, at):
        at += rows
        pv[at:at + v.shape[0], t * 128:t * 128 + 128] = v.astype(BF16)

    prep_body(rows, lambda t: near[:, t * 128:t * 128 + 128], put, lin[...], lout[...], fst[...], lst[...], rec[...], 16)
    part[...] = scores_of(tv[...], pv[...])


def bulk(own, near, mid, tv, maps):
    rows, f = own.shape
    n = tv.shape[0]
    return pl.pallas_call(
        bulk_kernel,
        out_shape=jax.ShapeDtypeStruct((2 * rows + 16, n), F32),
        in_specs=[VM] * 9,
        out_specs=VM,
        scratch_shapes=[pltpu.VMEM((2 * rows + 16, f), BF16)],
        **settings(3.5),
    )(own, near, mid, tv, *maps)


def last_kernel(mid2, far, far2, tv, part, mine, core, across, both, pv, sv):
    half = 16 * lax.axis_index("grp")
    other = 16 - half
    rows = mine.shape[0]
    slot = lax.axis_index("ex") ^ lax.axis_index("lyr")

    def at(m, extra, size):
        return pl.ds(pl.multiple_of((slot ^ m) * rows + extra, 16), size)

    sv[at(0, 0, rows), :] = part[0:rows, :]
    sv[at(1, 0, rows), :] = part[rows:2 * rows, :]
    sv[at(3, half, 16), :] = part[2 * rows:, :]
    for i, p in enumerate((mid2, far, far2)):
        pv[i * 16:i * 16 + 16, :] = p[...]
    late = scores_of(tv[...], pv[...])
    sv[at(3, other, 16), :] = late[0:16]
    sv[at(2, half, 16), :] = late[16:32]
    sv[at(2, other, 16), :] = late[32:48]
    for m, o in enumerate((mine, core, across, both)):
        o[...] = sv[m * rows:m * rows + rows, :].astype(o.dtype)


def final(mid2, far, far2, tv, part, rows):
    n, f = tv.shape
    return pl.pallas_call(
        last_kernel,
        out_shape=[jax.ShapeDtypeStruct((rows, n), d) for d in (F32, F32, SENT, SENT)],
        in_specs=[VM] * 5,
        out_specs=[VM] * 4,
        scratch_shapes=[pltpu.VMEM((48, f), BF16), pltpu.VMEM((4 * rows, n), F32)],
        **settings(1.3),
    )(mid2, far, far2, tv, part)


SENT = BF16


def flip(x, axis, mask, size):
    return lax.ppermute(x, axis, [(i, i ^ mask) for i in range(size)])


def plain(sizes, train, query, bo, bi, ev):
    g = query.shape[1]
    matrix = query[0].astype(F32).reshape(g, GR, GC)
    high = lax.Precision.HIGHEST
    x = jnp.einsum("ba,qbc->qac", bo[0], matrix, precision=high)
    x = jnp.einsum("qac,cd->qad", x, bi[0], precision=high)
    x = x / (ev.reshape(1, GR, GC) + damping)
    x = jnp.einsum("ab,qbc->qac", bo[0], x, precision=high)
    x = jnp.einsum("qac,dc->qad", x, bi[0], precision=high)
    ready = lax.all_gather(x.reshape(g, GR * GC).astype(BF16), "ex", axis=0, tiled=True)
    part = dot(train[0], ready, 1, 1)
    return lax.psum_scatter(part, "lyr", scatter_dimension=1, tiled=True) / math.sqrt(GR * GC)


def local(sizes, train, query, bo, bi, ev):
    if sizes != (4, 4, 2) or query.shape[1] != 32:
        return plain(sizes, train, query, bo, bi, ev)
    start = 16 * lax.axis_index("grp")
    half = lax.dynamic_slice_in_dim(query[0], start, 16, 0)
    mid = flip(half, "ex", 3, 4)
    near = flip(query[0], "ex", 1, 4)
    tv, own, *maps = first(query, bo, bi, ev, train)
    mid = following(mid, maps)
    mid2 = flip(mid, "grp", 1, 2)
    far = flip(mid, "ex", 1, 4)
    far2 = lax.ppermute(mid, ("grp", "ex"), [(g * 4 + z, (1 - g) * 4 + (z ^ 1)) for g in range(2) for z in range(4)])
    part = bulk(own, near, mid, tv, maps)
    mine, core, across, both = final(mid2, far, far2, tv, part, query.shape[1])
    total = mine + flip(core, "lyr", 1, 4)
    total = total + flip(across, "lyr", 2, 4).astype(F32) + flip(both, "lyr", 3, 4).astype(F32)
    return total.T


def solution(mesh):
    sizes = tuple(mesh.shape[a] for a in ("ex", "lyr", "grp"))
    return jax.shard_map(
        functools.partial(local, sizes),
        mesh=mesh,
        in_specs=(
            P("lyr", ("grp", "ex"), None),
            P("lyr", "ex", None),
            P("lyr", None, None),
            P("lyr", None, None),
            P("lyr", None),
        ),
        out_specs=P(("grp", "ex"), "lyr"),
        check_vma=False,
    )
```

```python
import functools
import math

import jax, jax.numpy as jnp
from jax import lax
from jax.experimental import pallas as pl
from jax.experimental.pallas import tpu as pltpu
from jax.sharding import PartitionSpec as P

GR = 64
GC = 64
damping = 0.1
F32, BF16 = jnp.float32, jnp.bfloat16
VM = pl.BlockSpec(memory_space=pltpu.VMEM)


def dot(a, b, ca=1, cb=0):
    return lax.dot_general(a, b, (((ca,), (cb,)), ((), ())), preferred_element_type=F32)
def split(x):
    h = x.astype(BF16)
    return h, (x - h.astype(F32)).astype(BF16)
def selector(rows, which, swap):
    k = lax.broadcasted_iota(jnp.int32, (rows, 64), 0)
    b = lax.broadcasted_iota(jnp.int32, (rows, 64), 1)
    kk = k % 64
    par = kk // 32
    if swap: par = 1 - par
    hit = b == 2 * (kk % 32) + par
    if which == 1: hit = hit & (k < 128)
    if which == 2: hit = hit & (k >= 128)
    return jnp.where(hit, 1.0, 0.0).astype(BF16)
def row_maps(bo):
    h, l = split(bo)
    sel = selector(64, 0, False)
    outs = []
    for cb in (1, 0):
        th, tl = dot(sel, h, 1, cb).astype(BF16), dot(sel, l, 1, cb).astype(BF16)
        parts = []
        for swap in (False, True):
            full = dot(th, selector(192, 1, swap), 1, 1) + dot(tl, selector(192, 2, swap), 1, 1)
            parts.append(full[32 * swap:32 * swap + 32])
        outs.append(jnp.concatenate(parts, 0).astype(BF16))
    return outs
def col_maps(bi):
    h, l = split(bi)
    r = lax.broadcasted_iota(jnp.int32, (128, 64), 0) % 64
    c = lax.broadcasted_iota(jnp.int32, (128, 64), 1)
    e = jnp.where(r == c, 1.0, 0.0).astype(BF16)
    i = lax.broadcasted_iota(jnp.int32, (128, 128), 0) // 64
    j = lax.broadcasted_iota(jnp.int32, (128, 128), 1) // 64
    same = i == j
    def tile(x, cb):
        t = dot(e, x, 1, cb).astype(BF16)
        return dot(t, e, 1, 1)
    def pick(t, m): return jnp.where(m, t, 0.0).astype(BF16)
    th, tl = tile(h, 0), tile(l, 0)
    diff = jnp.logical_not(same)
    first = jnp.concatenate([jnp.concatenate([pick(th, same), pick(th, diff)], 1), jnp.concatenate([pick(tl, same), pick(tl, diff)], 1)], 0)
    uh, ul = tile(h, 1), tile(l, 1)
    last = jnp.concatenate([pick(uh, same), pick(uh, same), pick(ul, same)], 0)
    return first, last
def prep_body(nq, get, put, left_in, left_out, first, last, rec, group=16):
    g = jnp.concatenate([get(t) for t in range(32)], 0)
    x = dot(jnp.concatenate([g, g], 1), first)
    both = [jnp.swapaxes(v.reshape(32, nq, 128), 0, 1) for v in (x[:, :128], x[:, 128:])]
    lane = lax.broadcasted_iota(jnp.int32, (32, 128), 1) < 64
    for q0 in range(0, nq, group):
        qs = range(q0, q0 + group)
        ww = jnp.concatenate([jnp.concatenate([r[q] for q in qs], 1) for r in both], 0)
        h, l = split(ww)
        r = dot(left_in, jnp.concatenate([h, l, h], 0))
        ys, yr = [], []
        for i in range(group):
            s = slice(i * 128, i * 128 + 128)
            y = jnp.where(lane, r[:32, s], r[32:, s]) * rec
            ys.append(y); yr.append(pltpu.roll(y, 64, 1))
        yy = jnp.concatenate([jnp.concatenate(ys, 1), jnp.concatenate(yr, 1)], 0)
        h, l = split(yy)
        r = dot(left_out, jnp.concatenate([h, l, h], 0))
        z = jnp.concatenate([jnp.where(lane, r[:32, i * 128:i * 128 + 128], r[32:, i * 128:i * 128 + 128]) for i in range(group)], 0)
        h, l = split(z)
        o = dot(jnp.concatenate([h, l, h], 1), last)
        o = jnp.swapaxes(o.reshape(group, 32, 128), 0, 1)
        for t in range(32):
            put(t, o[t], q0)

def scores_of(train, ready):
    return dot(train, ready, 1, 1).T * (1.0 / math.sqrt(GR * GC))


def first_kernel(nq, q_hbm, bo_hbm, bi_hbm, ev_hbm, train_hbm, tv, out, lin, lout, fst, lst, rec, qv, bov, biv, evv, sem):
    copies = [
        pltpu.make_async_copy(a, b, sem.at[i])
        for i, (a, b) in enumerate(((bo_hbm, bov), (bi_hbm, biv), (ev_hbm, evv), (q_hbm, qv), (train_hbm.at[0], tv)))
    ]
    for c in copies:
        c.start()
    for c in copies[:4]:
        c.wait()
    for t in range(32):
        rec[t:t + 1, :] = 1.0 / (evv[0:1, t * 128:t * 128 + 128] + damping)
    lin[...], lout[...] = row_maps(bov[0])
    fst[...], lst[...] = col_maps(biv[0])

    def put(t, v, at):
        out[at:at + v.shape[0], t * 128:t * 128 + 128] = v.astype(BF16)

    prep_body(nq, lambda t: qv[0, :, t * 128:t * 128 + 128], put, lin[...], lout[...], fst[...], lst[...], rec[...], 16)
    copies[4].wait()


def maps_shapes():
    return [
        jax.ShapeDtypeStruct((64, 192), BF16),
        jax.ShapeDtypeStruct((64, 192), BF16),
        jax.ShapeDtypeStruct((256, 256), BF16),
        jax.ShapeDtypeStruct((384, 128), BF16),
        jax.ShapeDtypeStruct((32, 128), F32),
    ]


def settings(us):
    return dict(
        compiler_params=pltpu.CompilerParams(vmem_limit_bytes=20 << 20),
        cost_estimate=pl.CostEstimate(flops=int(us * 1e9), bytes_accessed=int(us * 3.6e6), transcendentals=0),
    )


def first(*args):
    q, bo, bi, ev, train = args
    nq = q.shape[1]
    return pl.pallas_call(
        functools.partial(first_kernel, nq),
        out_shape=[jax.ShapeDtypeStruct(x.shape[1:], BF16) for x in (train, q)] + maps_shapes(),
        in_specs=[pl.BlockSpec(memory_space=pltpu.HBM)] * 5,
        out_specs=[VM] * 7,
        scratch_shapes=[pltpu.VMEM(q.shape, BF16)]
        + [pltpu.VMEM(x.shape, F32) for x in (bo, bi, ev)]
        + [pltpu.SemaphoreType.DMA((5,))],
        **settings(4),
    )(*(pltpu.with_memory_space_constraint(x, pltpu.HBM) for x in args))


def next_kernel(nq, chunk, lin, lout, fst, lst, rec, out):
    def put(t, v, at):
        out[at:at + v.shape[0], t * 128:t * 128 + 128] = v.astype(BF16)

    prep_body(nq, lambda t: chunk[:, t * 128:t * 128 + 128], put, lin[...], lout[...], fst[...], lst[...], rec[...], 16)


def following(chunk, maps):
    nq = chunk.shape[0]
    return pl.pallas_call(
        functools.partial(next_kernel, nq),
        out_shape=jax.ShapeDtypeStruct(chunk.shape, BF16),
        in_specs=[VM] * 6,
        out_specs=VM,
        **settings(nq / 12),
    )(chunk, *maps)


def bulk_kernel(own, near, mid, tv, lin, lout, fst, lst, rec, part, pv):
    rows = own.shape[0]
    pv[0:rows, :] = own[...]
    pv[2 * rows:, :] = mid[...]

    def put(t, v, at):
        at += rows
        pv[at:at + v.shape[0], t * 128:t * 128 + 128] = v.astype(BF16)

    prep_body(rows, lambda t: near[:, t * 128:t * 128 + 128], put, lin[...], lout[...], fst[...], lst[...], rec[...], 16)
    half = 16 * lax.axis_index("grp")
    slot = lax.axis_index("ex") ^ lax.axis_index("lyr")

    def at(m, extra, size):
        return pl.ds(pl.multiple_of((slot ^ m) * rows + extra, 16), size)

    early = scores_of(tv[...], pv[...])
    part[at(0, 0, rows), :] = early[0:rows]
    part[at(1, 0, rows), :] = early[rows:2 * rows]
    part[at(3, half, 16), :] = early[2 * rows:]


def bulk(own, near, mid, tv, maps):
    rows, f = own.shape
    n = tv.shape[0]
    return pl.pallas_call(
        bulk_kernel,
        out_shape=jax.ShapeDtypeStruct((4 * rows, n), F32),
        in_specs=[VM] * 9,
        out_specs=VM,
        scratch_shapes=[pltpu.VMEM((2 * rows + 16, f), BF16)],
        **settings(3.5),
    )(own, near, mid, tv, *maps)


def last_kernel(mid2, far, far2, tv, part, mine, core, across, both, sv):
    half = 16 * lax.axis_index("grp")
    other = 16 - half
    rows = mine.shape[0]
    slot = lax.axis_index("ex") ^ lax.axis_index("lyr")

    def at(m, extra, size):
        return pl.ds(pl.multiple_of((slot ^ m) * rows + extra, 16), size)

    late = scores_of(tv[...], jnp.concatenate([p[...] for p in (mid2, far, far2)], 0))
    sv[...] = part[...]
    sv[at(3, other, 16), :] = late[0:16]
    sv[at(2, half, 16), :] = late[16:32]
    sv[at(2, other, 16), :] = late[32:48]
    for m, o in enumerate((mine, core, across, both)):
        o[...] = sv[m * rows:m * rows + rows, :].astype(o.dtype)


def final(mid2, far, far2, tv, part, rows):
    n, f = tv.shape
    return pl.pallas_call(
        last_kernel,
        out_shape=[jax.ShapeDtypeStruct((rows, n), d) for d in (F32, F32, SENT, SENT)],
        in_specs=[VM] * 5,
        out_specs=[VM] * 4,
        scratch_shapes=[pltpu.VMEM((4 * rows, n), F32)],
        **settings(1.3),
    )(mid2, far, far2, tv, part)


SENT = BF16


def flip(x, axis, mask, size):
    return lax.ppermute(x, axis, [(i, i ^ mask) for i in range(size)])


def plain(sizes, train, query, bo, bi, ev):
    g = query.shape[1]
    matrix = query[0].astype(F32).reshape(g, GR, GC)
    high = lax.Precision.HIGHEST
    x = jnp.einsum("ba,qbc->qac", bo[0], matrix, precision=high)
    x = jnp.einsum("qac,cd->qad", x, bi[0], precision=high)
    x = x / (ev.reshape(1, GR, GC) + damping)
    x = jnp.einsum("ab,qbc->qac", bo[0], x, precision=high)
    x = jnp.einsum("qac,dc->qad", x, bi[0], precision=high)
    ready = lax.all_gather(x.reshape(g, GR * GC).astype(BF16), "ex", axis=0, tiled=True)
    part = dot(train[0], ready, 1, 1)
    return lax.psum_scatter(part, "lyr", scatter_dimension=1, tiled=True) / math.sqrt(GR * GC)


def local(sizes, train, query, bo, bi, ev):
    if sizes != (4, 4, 2) or query.shape[1] != 32:
        return plain(sizes, train, query, bo, bi, ev)
    start = 16 * lax.axis_index("grp")
    half = lax.dynamic_slice_in_dim(query[0], start, 16, 0)
    mid = flip(half, "ex", 3, 4)
    near = flip(query[0], "ex", 1, 4)
    tv, own, *maps = first(query, bo, bi, ev, train)
    mid = following(mid, maps)
    mid2 = flip(mid, "grp", 1, 2)
    far = flip(mid, "ex", 1, 4)
    far2 = lax.ppermute(mid, ("grp", "ex"), [(g * 4 + z, (1 - g) * 4 + (z ^ 1)) for g in range(2) for z in range(4)])
    part = bulk(own, near, mid, tv, maps)
    mine, core, across, both = final(mid2, far, far2, tv, part, query.shape[1])
    total = mine + flip(core, "lyr", 1, 4)
    total = total + flip(across, "lyr", 2, 4).astype(F32) + flip(both, "lyr", 3, 4).astype(F32)
    return total.T


def solution(mesh):
    sizes = tuple(mesh.shape[a] for a in ("ex", "lyr", "grp"))
    return jax.shard_map(
        functools.partial(local, sizes),
        mesh=mesh,
        in_specs=(
            P("lyr", ("grp", "ex"), None),
            P("lyr", "ex", None),
            P("lyr", None, None),
            P("lyr", None, None),
            P("lyr", None),
        ),
        out_specs=P(("grp", "ex"), "lyr"),
        check_vma=False,
    )
```
